32 devices in a mesh: ctx: 4 (over z), head: 8 (over y, x, core).
Axes of the slice: x: 2, y: 2, z: 4, core: 2. Of those that a mesh axis runs over, the one named last changes fastest.
Arguments:
- queries: bfloat16 [4096, 24576], P('ctx', 'head'), may hold values from -110 to 110
- latent_kv: bfloat16 [4096, 576], P('ctx'), may hold values from -6 to 6
- w_uk: bfloat16 [128, 512, 128], P('head'), may hold values from -0.25 to 0.25
- w_uv: bfloat16 [128, 512, 128], P('head'), may hold values from -0.25 to 0.25
- grad_out: bfloat16 [4096, 16384], P('ctx', 'head'), may hold values from -48 to 48
Outputs:
- grad_queries: bfloat16 [4096, 24576], P('ctx', 'head')
- grad_latent: float32 [4096, 576], P(('ctx', 'head'))
The draws below stay inside these ranges and needn't reach their ends.
All inputs are finite; a program needn't handle non-finite values.
Results may differ from the reference program's by a relative error of at most 0.013.
Values may be sent and summed in bfloat16 or wider, within the bound.
A program may use at most 192 MiB of HBM per device.

```python
import jax
import jax.numpy as jnp
from jax import lax

HEADS = 128
DN = 128
DR = 64
DV = 128
DL = 512
W = 512
TOKENS = 4096


def latent_rows_draw(key):
    base = jax.random.fold_in(key, 11)
    latent = jnp.clip(jax.random.normal(base, (TOKENS, DL + DR), jnp.float32), -6.0, 6.0)
    return latent


def draw_latent_kv(key, part):
    return latent_rows_draw(key).astype(jnp.bfloat16)


def draw_queries(key, part):
    base = jax.random.fold_in(key, 23)
    random_example = jnp.clip(jax.random.normal(base, (TOKENS, HEADS, DN + DR), jnp.float32), -6.0, 6.0)
    return random_example.reshape(TOKENS, HEADS * (DN + DR)).astype(jnp.bfloat16)


def steps_of(stream_key, shape, cuts, low, largest):
    def one(position, shards_of):
        draws = jax.random.uniform(jax.random.fold_in(jax.random.fold_in(stream_key, 6), position), (shards_of,), jnp.float32, low / len(cuts), largest / len(cuts))
        return jnp.repeat(jnp.exp(draws), shape[position] // shards_of).reshape((-1,) + (1,) * (len(shape) - position - 1))

    gain = one(*cuts[0])
    for cut in cuts[1:]:
        gain = gain * one(*cut)
    return gain


def bell_draw(rng, shape, deviation, reach, shards=(), kind=jnp.bfloat16):
    array = deviation * jax.random.normal(rng, shape, jnp.float32)
    if shards:
        array = array * steps_of(rng, shape, shards, -0.22, 0.18)
    return jnp.clip(array, -reach, reach).astype(kind)


def setup_inputs(seed: int = 0) -> dict:
    streams_of = jax.random.split(jax.random.key(seed), 6)
    queries = draw_queries(jax.random.fold_in(streams_of[5], 71), 0)
    latent_kv = draw_latent_kv(jax.random.fold_in(streams_of[5], 71), 0)
    w_uk = bell_draw(streams_of[2], (HEADS, DL, DN), DL ** -0.5, 0.25, ((0, 8),))
    w_uv = bell_draw(streams_of[3], (HEADS, DL, DV), DL ** -0.5, 0.25, ((0, 8),))
    grad_out = bell_draw(streams_of[4], (TOKENS, HEADS * DV), 8.0, 48.0, ((0, 4), (1, 8)))
    return dict(queries=queries, latent_kv=latent_kv, w_uk=w_uk, w_uv=w_uv, grad_out=grad_out)


def windows(array_in, block_count):
    zeros_pad = jnp.zeros((W,) + array_in.shape[1:], array_in.dtype)
    padded = jnp.concatenate([zeros_pad, array_in], axis=0)
    lower_part = padded[:-W].reshape((block_count, W) + array_in.shape[1:])
    upper_part = padded[W:].reshape((block_count, W) + array_in.shape[1:])
    return jnp.concatenate([lower_part, upper_part], axis=1)


def fold_window_back(window_terms, row_total_count):
    tail_shape = window_terms.shape[2:]
    lower_part = window_terms[:, :W].reshape((row_total_count,) + tail_shape)
    upper_part = window_terms[:, W:].reshape((row_total_count,) + tail_shape)
    shifted = jnp.concatenate([lower_part[W:], jnp.zeros((W,) + tail_shape, jnp.float32)], axis=0)
    return upper_part + shifted


def reference(queries, latent_kv, w_uk, w_uv, grad_out):
    row_total_count = queries.shape[0]
    block_count = row_total_count // W
    query_dim = DN + DR
    score_scale = query_dim ** -0.5
    query_rows = queries.reshape(row_total_count, HEADS, query_dim)
    grad_rows = grad_out.reshape(row_total_count, HEADS, DV)
    latent_part = latent_kv[:, :DL]
    banded_positional_part = windows(latent_kv[:, DL:], block_count).astype(jnp.float32)
    lower_idx = jnp.arange(W)[:, None]
    upper_idx = jnp.arange(2 * W)[None, :]
    band = (upper_idx > lower_idx) & (upper_idx <= lower_idx + W)
    block_idx = jnp.arange(block_count)[:, None, None]
    allowed = band[None] & ((block_idx > 0) | (upper_idx[None] >= W))

    def head_step(accum, head):
        keys_nope = jnp.dot(latent_part, w_uk[head], preferred_element_type=jnp.float32).astype(jnp.bfloat16)
        values = jnp.dot(latent_part, w_uv[head], preferred_element_type=jnp.float32).astype(jnp.bfloat16)
        windowed_keys = windows(keys_nope, block_count).astype(jnp.float32)
        windowed_values = windows(values, block_count).astype(jnp.float32)
        query_head = query_rows[:, head].reshape(block_count, W, query_dim).astype(jnp.float32)
        query_unrotated = query_head[:, :, :DN]
        query_rotary = query_head[:, :, DN:]
        head_gradient = grad_rows[:, head].reshape(block_count, W, DV).astype(jnp.float32)
        logit_scores = jnp.einsum("rpm,rsm->rps", query_unrotated, windowed_keys) + jnp.einsum("zvp,zhp->zvh", query_rotary, banded_positional_part)
        logit_scores = jnp.where(allowed, logit_scores * score_scale, -jnp.inf)
        peak = jnp.max(logit_scores, axis=2, keepdims=True)
        expo = jnp.exp(logit_scores - peak)
        probs = expo / jnp.sum(expo, axis=2, keepdims=True)
        lowered_probabilities = lax.optimization_barrier(probs.astype(jnp.bfloat16)).astype(jnp.float32)
        attended_output = jnp.einsum("swa,sao->swo", lowered_probabilities, windowed_values)
        delta = jnp.sum(head_gradient * attended_output, axis=2)
        probability_gradient = jnp.einsum("olj,oaj->ola", head_gradient, windowed_values)
        similarity_derivative = probs * (probability_gradient - delta[:, :, None])
        similarity_derivative = lax.optimization_barrier(similarity_derivative.astype(jnp.bfloat16)).astype(jnp.float32)
        unrotated_gradient = jnp.einsum("fyg,fgr->fyr", similarity_derivative, windowed_keys)
        positional_request_derivative = jnp.einsum("zcg,zgy->zcy", similarity_derivative, banded_positional_part)
        grad_query = (jnp.concatenate([unrotated_gradient, positional_request_derivative], axis=2) * score_scale).astype(jnp.bfloat16)
        key_gradient = fold_window_back(jnp.einsum("fjg,fjl->fgl", similarity_derivative, query_unrotated) * score_scale, row_total_count)
        value_gradient = fold_window_back(jnp.einsum("ytn,ytc->ync", lowered_probabilities, head_gradient), row_total_count)
        rotary_gradient = fold_window_back(jnp.einsum("pyj,pyl->pjl", similarity_derivative, query_rotary) * score_scale, row_total_count)
        latent_grad = jnp.dot(key_gradient, w_uk[head].astype(jnp.float32).T, precision=lax.Precision.HIGHEST)
        latent_grad = latent_grad + jnp.dot(value_gradient, w_uv[head].astype(jnp.float32).T, precision=lax.Precision.HIGHEST)
        accum = accum + jnp.concatenate([latent_grad, rotary_gradient], axis=1)
        return accum, grad_query.reshape(row_total_count, query_dim)

    start_accum = jnp.zeros((row_total_count, DL + DR), jnp.float32)
    grad_latent, per_head = lax.scan(head_step, start_accum, jnp.arange(HEADS, dtype=jnp.int32))
    grad_queries = jnp.transpose(per_head, (1, 0, 2)).reshape(row_total_count, HEADS * query_dim)
    return grad_queries, grad_latent
```

```python
import functools
import math

import jax
import jax.numpy as jnp
from jax import lax
from jax.experimental import pallas as pl
from jax.experimental.pallas import tpu as pltpu
from jax.sharding import PartitionSpec as P

W = 512
T = 256
NEG = -1e30
NT = (((1,), (1,)), ((), ()))
NN = (((1,), (0,)), ((), ()))


def mm(a, b, dims=NN):
    return lax.dot_general(a, b, dims, preferred_element_type=jnp.float32)


def attend_kernel(
    prev_ref, own_ref, q_ref, uk_ref, uv_ref, g_ref, gq_ref, part_ref,
    kcat, kt, vs, pt, dst, acc, racc,
):
    step = pl.program_id(0)
    tokens = q_ref.shape[0]
    tiles = tokens // T
    reach = W // T
    chunks = tiles + reach
    dl = uk_ref.shape[1]
    scale = 192 ** -0.5
    c2 = scale * math.log2(math.e)
    first_bias = jnp.where(lax.axis_index("ctx") == 0, NEG, 0.0).astype(jnp.float32)

    @pl.when(step == 0)
    def _():
        acc[...] = jnp.zeros_like(acc)
        racc[...] = jnp.zeros_like(racc)

    wk = jnp.concatenate([uk_ref[0], uk_ref[1]], axis=1)
    wv = jnp.concatenate([uv_ref[0], uv_ref[1]], axis=1)
    wall = jnp.concatenate([wk, wv], axis=1)
    zero64 = jnp.zeros((T, 64), jnp.float32)
    zero128 = jnp.zeros((T, 128), jnp.float32)

    for j in range(chunks):
        rows = slice(j * T, (j + 1) * T)
        if j < reach:
            lat = prev_ref[j * T:(j + 1) * T, :]
        else:
            lat = own_ref[(j - reach) * T:(j - reach + 1) * T, :]
        kr = lat[:, dl:].astype(jnp.float32)
        k2 = mm(lat[:, :dl], wk)
        v2 = mm(lat[:, :dl], wv)
        ka = jnp.concatenate([k2[:, :128], kr, zero64], axis=1).astype(jnp.bfloat16)
        kb = pltpu.roll(jnp.concatenate([k2[:, 128:], kr, zero64], axis=1), 64, 1).astype(jnp.bfloat16)
        kcat[0, rows, :] = ka
        kcat[1, rows, :] = kb
        kt[0, :, rows] = ka.T
        kt[1, :, rows] = kb.T
        vs[rows, :] = v2.astype(jnp.bfloat16)

    u = lax.broadcasted_iota(jnp.int32, (T, T), 0)
    r = lax.broadcasted_iota(jnp.int32, (T, T), 1)
    low_keep = u > r
    lane = lax.broadcasted_iota(jnp.int32, (T, 128), 1)

    def tile(t, e):
        qrows = slice(t * T, (t + 1) * T)
        q = q_ref[qrows, e * 128:e * 128 + 256]
        g = g_ref[qrows, e * 128:e * 128 + 128]
        ss = []
        for a in range(reach + 1):
            rows = slice((t + a) * T, (t + a + 1) * T)
            s = mm(kcat[e, rows, :], q, NT)
            if a == 0:
                s = jnp.where(low_keep, s, NEG)
            if a == reach:
                s = jnp.where(low_keep, NEG, s)
            if t + a < reach:
                s = s + first_bias
            ss.append(s)
        peak = jnp.max(ss[0], axis=0, keepdims=True)
        for s in ss[1:]:
            peak = jnp.maximum(peak, jnp.max(s, axis=0, keepdims=True))
        es = [jnp.exp2((s - peak) * c2) for s in ss]
        total = sum(jnp.sum(x, axis=0, keepdims=True) for x in es)
        inv = 1.0 / total
        ds_list = []
        dps = []
        delta = jnp.zeros((1, T), jnp.float32)
        for a in range(reach + 1):
            rows = slice((t + a) * T, (t + a + 1) * T)
            dp = mm(vs[rows, e * 128:e * 128 + 128], g, NT)
            dps.append(dp)
            delta = delta + jnp.sum(es[a] * dp, axis=0, keepdims=True)
        delta = delta * inv
        dq = jnp.zeros((256, T), jnp.float32)
        for a in range(reach + 1):
            rows = slice((t + a) * T, (t + a + 1) * T)
            p = es[a] * inv
            pt[e, rows, qrows] = p.astype(jnp.bfloat16)
            ds = (p * (dps[a] - delta)).astype(jnp.bfloat16)
            dst[e, rows, qrows] = ds
            ds_list.append(ds)
        dq = mm(kt[e, :, t * T:(t + reach + 1) * T], jnp.concatenate(ds_list, axis=0))
        return (dq * scale).T

    def chunk(j):
        rows = slice(j * T, (j + 1) * T)
        t0, t1 = max(0, j - reach), min(tiles - 1, j)
        qrows = slice(t0 * T, (t1 + 1) * T)
        dka = mm(dst[0, rows, qrows], q_ref[qrows, 0:256]) * scale
        dkb = mm(dst[1, rows, qrows], q_ref[qrows, 128:384]) * scale
        dva = mm(pt[0, rows, qrows], g_ref[qrows, 0:128])
        dvb = mm(pt[1, rows, qrows], g_ref[qrows, 128:256])
        racc[rows, :] += jnp.where(lane < 64, dka[:, 128:], dkb[:, 128:])
        dkb = pltpu.roll(dkb, 192, 1)[:, :128]
        grads = jnp.concatenate(
            [dka[:, :128], dkb, dva, dvb], axis=1
        ).astype(jnp.bfloat16)
        acc[rows, :] += mm(grads, wall, NT)

    for t in range(tiles):
        qrows = slice(t * T, (t + 1) * T)
        a = tile(t, 0)
        b = tile(t, 1)
        gq_ref[qrows, 0:128] = a[:, :128].astype(jnp.bfloat16)
        gq_ref[qrows, 128:256] = (a[:, 128:] + b[:, :128]).astype(jnp.bfloat16)
        gq_ref[qrows, 256:384] = b[:, 128:].astype(jnp.bfloat16)
        chunk(t)
    for j in range(tiles, chunks):
        chunk(j)

    @pl.when(step == pl.num_programs(0) - 1)
    def _():
        part_ref[:, :dl] = acc[...].astype(part_ref.dtype)
        part_ref[:, dl:] = (racc[:, :64] + racc[:, 64:]).astype(part_ref.dtype)


def attend(previous, latent_kv, queries, w_uk, w_uv, grad_out):
    tokens = queries.shape[0]
    heads = w_uk.shape[0]
    dl = w_uk.shape[1]
    rows = tokens + W
    width = latent_kv.shape[1]
    full = lambda s: pl.BlockSpec(s, lambda i: (0,) * len(s))
    return pl.pallas_call(
        attend_kernel,
        grid=(heads // 2,),
        in_specs=[
            full(previous.shape),
            full(latent_kv.shape),
            pl.BlockSpec((tokens, 384), lambda i: (0, i)),
            pl.BlockSpec((2, dl, 128), lambda i: (i, 0, 0)),
            pl.BlockSpec((2, dl, 128), lambda i: (i, 0, 0)),
            pl.BlockSpec((tokens, 256), lambda i: (0, i)),
        ],
        out_specs=[
            pl.BlockSpec((tokens, 384), lambda i: (0, i)),
            full((rows, width)),
        ],
        out_shape=[
            jax.ShapeDtypeStruct(queries.shape, jnp.bfloat16),
            jax.ShapeDtypeStruct((rows, width), jnp.float32),
        ],
        scratch_shapes=[
            pltpu.VMEM((2, rows, 256), jnp.bfloat16),
            pltpu.VMEM((2, 256, rows), jnp.bfloat16),
            pltpu.VMEM((rows, 256), jnp.bfloat16),
            pltpu.VMEM((2, rows, tokens), jnp.bfloat16),
            pltpu.VMEM((2, rows, tokens), jnp.bfloat16),
            pltpu.VMEM((rows, dl), jnp.float32),
            pltpu.VMEM((rows, 128), jnp.float32),
        ],
        compiler_params=pltpu.CompilerParams(vmem_limit_bytes=56 * 2 ** 20),
    )(previous, latent_kv, queries, w_uk, w_uv, grad_out)


def shift(array, axis, by):
    peers = lax.axis_size(axis)
    return lax.ppermute(array, axis, [(i, i + by) for i in range(peers) if 0 <= i + by < peers])


def shards(queries, latent_kv, w_uk, w_uv, grad_out):
    tokens = queries.shape[0]
    previous = shift(latent_kv[tokens - W:], "ctx", 1)
    grad_queries, part = attend(previous, latent_kv, queries, w_uk, w_uv, grad_out)
    returned = shift(part[:W].astype(jnp.bfloat16), "ctx", -1).astype(jnp.float32)
    extra = jnp.concatenate(
        [jnp.zeros((tokens - W, part.shape[1]), jnp.float32), returned], axis=0
    )
    grad_latent = lax.psum_scatter(part[W:] + extra, "head", scatter_dimension=0, tiled=True)
    return grad_queries, grad_latent


def solution(mesh):
    in_specs = (
        P("ctx", "head"),
        P("ctx", None),
        P("head", None, None),
        P("head", None, None),
        P("ctx", "head"),
    )
    out_specs = (P("ctx", "head"), P(("ctx", "head"), None))
    return jax.shard_map(shards, mesh=mesh, in_specs=in_specs, out_specs=out_specs, check_vma=False)
```

```python
import functools
import math

import jax
import jax.numpy as jnp
from jax import lax
from jax.experimental import pallas as pl
from jax.experimental.pallas import tpu as pltpu
from jax.sharding import PartitionSpec as P

W = 512
T = 256
NEG = -1e30
NT = (((1,), (1,)), ((), ()))
NN = (((1,), (0,)), ((), ()))


def mm(a, b, dims=NN):
    return lax.dot_general(a, b, dims, preferred_element_type=jnp.float32)


def attend_kernel(
    prev_ref, own_ref, q_ref, uk_ref, uv_ref, g_ref, gq_ref, part_ref,
    kcat, kt, vs, pt, dst, acc, racc, lats,
):
    step = pl.program_id(0)
    tokens = q_ref.shape[0]
    tiles = tokens // T
    reach = W // T
    chunks = tiles + reach
    dl = uk_ref.shape[1]
    scale = 192 ** -0.5
    c2 = scale * math.log2(math.e)
    first_bias = jnp.where(lax.axis_index("ctx") == 0, NEG, 0.0).astype(jnp.float32)

    @pl.when(step == 0)
    def _():
        acc[...] = jnp.zeros_like(acc)
        racc[...] = jnp.zeros_like(racc)
        for j in range(chunks):
            ref, i = (prev_ref, j) if j < reach else (own_ref, j - reach)
            lats[j * T:(j + 1) * T, :] = ref[:, i * T:(i + 1) * T].T

    wk = jnp.concatenate([uk_ref[0], uk_ref[1]], axis=1)
    wv = jnp.concatenate([uv_ref[0], uv_ref[1]], axis=1)
    wall = jnp.concatenate([wk, wv], axis=1)
    zero64 = jnp.zeros((T, 64), jnp.float32)
    zero128 = jnp.zeros((T, 128), jnp.float32)

    for j in range(chunks):
        rows = slice(j * T, (j + 1) * T)
        lat = lats[rows, :]
        kr = lat[:, dl:].astype(jnp.float32)
        k2 = mm(lat[:, :dl], wk)
        v2 = mm(lat[:, :dl], wv)
        ka = jnp.concatenate([k2[:, :128], kr, zero64], axis=1).astype(jnp.bfloat16)
        kb = pltpu.roll(jnp.concatenate([k2[:, 128:], kr, zero64], axis=1), 64, 1).astype(jnp.bfloat16)
        kcat[0, rows, :] = ka
        kcat[1, rows, :] = kb
        kt[0, :, rows] = ka.T
        kt[1, :, rows] = kb.T
        vs[rows, :] = v2.astype(jnp.bfloat16)

    u = lax.broadcasted_iota(jnp.int32, (T, T), 0)
    r = lax.broadcasted_iota(jnp.int32, (T, T), 1)
    low_keep = u > r
    lane = lax.broadcasted_iota(jnp.int32, (T, 128), 1)

    def tile(t, e):
        qrows = slice(t * T, (t + 1) * T)
        q = q_ref[qrows, e * 128:e * 128 + 256]
        g = g_ref[qrows, e * 128:e * 128 + 128]
        ss = []
        for a in range(reach + 1):
            rows = slice((t + a) * T, (t + a + 1) * T)
            s = mm(kcat[e, rows, :], q, NT)
            if a == 0:
                s = jnp.where(low_keep, s, NEG)
            if a == reach:
                s = jnp.where(low_keep, NEG, s)
            if t + a < reach:
                s = s + first_bias
            ss.append(s)
        peak = jnp.max(ss[0], axis=0, keepdims=True)
        for s in ss[1:]:
            peak = jnp.maximum(peak, jnp.max(s, axis=0, keepdims=True))
        es = [jnp.exp2((s - peak) * c2) for s in ss]
        total = sum(jnp.sum(x, axis=0, keepdims=True) for x in es)
        inv = 1.0 / total
        ds_list = []
        dps = []
        delta = jnp.zeros((1, T), jnp.float32)
        for a in range(reach + 1):
            rows = slice((t + a) * T, (t + a + 1) * T)
            dp = mm(vs[rows, e * 128:e * 128 + 128], g, NT)
            dps.append(dp)
            delta = delta + jnp.sum(es[a] * dp, axis=0, keepdims=True)
        delta = delta * inv
        dq = jnp.zeros((256, T), jnp.float32)
        for a in range(reach + 1):
            rows = slice((t + a) * T, (t + a + 1) * T)
            p = es[a] * inv
            pt[e, rows, qrows] = p.astype(jnp.bfloat16)
            ds = (p * (dps[a] - delta)).astype(jnp.bfloat16)
            dst[e, rows, qrows] = ds
            ds_list.append(ds)
        dq = mm(kt[e, :, t * T:(t + reach + 1) * T], jnp.concatenate(ds_list, axis=0))
        return (dq * scale).T

    def chunk(j):
        rows = slice(j * T, (j + 1) * T)
        t0, t1 = max(0, j - reach), min(tiles - 1, j)
        qrows = slice(t0 * T, (t1 + 1) * T)
        dka = mm(dst[0, rows, qrows], q_ref[qrows, 0:256]) * scale
        dkb = mm(dst[1, rows, qrows], q_ref[qrows, 128:384]) * scale
        dva = mm(pt[0, rows, qrows], g_ref[qrows, 0:128])
        dvb = mm(pt[1, rows, qrows], g_ref[qrows, 128:256])
        racc[rows, :] += jnp.where(lane < 64, dka[:, 128:], dkb[:, 128:])
        dkb = pltpu.roll(dkb, 192, 1)[:, :128]
        grads = jnp.concatenate(
            [dka[:, :128], dkb, dva, dvb], axis=1
        ).astype(jnp.bfloat16)
        acc[rows, :] += mm(grads, wall, NT)

    for t in range(tiles):
        qrows = slice(t * T, (t + 1) * T)
        a = tile(t, 0)
        b = tile(t, 1)
        gq_ref[qrows, 0:128] = a[:, :128].astype(jnp.bfloat16)
        gq_ref[qrows, 128:256] = (a[:, 128:] + b[:, :128]).astype(jnp.bfloat16)
        gq_ref[qrows, 256:384] = b[:, 128:].astype(jnp.bfloat16)
        chunk(t)
    for j in range(tiles, chunks):
        chunk(j)

    @pl.when(step == pl.num_programs(0) - 1)
    def _():
        part_ref[:, :dl] = acc[...].astype(part_ref.dtype)
        part_ref[:, dl:] = (racc[:, :64] + racc[:, 64:]).astype(part_ref.dtype)


def attend(previous, latent_kv, queries, w_uk, w_uv, grad_out):
    tokens = queries.shape[0]
    heads = w_uk.shape[0]
    dl = w_uk.shape[1]
    rows = tokens + W
    width = latent_kv.shape[0]
    full = lambda s: pl.BlockSpec(s, lambda i: (0,) * len(s))
    return pl.pallas_call(
        attend_kernel,
        grid=(heads // 2,),
        in_specs=[
            full(previous.shape),
            full(latent_kv.shape),
            pl.BlockSpec((tokens, 384), lambda i: (0, i)),
            pl.BlockSpec((2, dl, 128), lambda i: (i, 0, 0)),
            pl.BlockSpec((2, dl, 128), lambda i: (i, 0, 0)),
            pl.BlockSpec((tokens, 256), lambda i: (0, i)),
        ],
        out_specs=[
            pl.BlockSpec((tokens, 384), lambda i: (0, i)),
            full((rows, width)),
        ],
        out_shape=[
            jax.ShapeDtypeStruct(queries.shape, jnp.bfloat16),
            jax.ShapeDtypeStruct((rows, width), jnp.bfloat16),
        ],
        scratch_shapes=[
            pltpu.VMEM((2, rows, 256), jnp.bfloat16),
            pltpu.VMEM((2, 256, rows), jnp.bfloat16),
            pltpu.VMEM((rows, 256), jnp.bfloat16),
            pltpu.VMEM((2, rows, tokens), jnp.bfloat16),
            pltpu.VMEM((2, rows, tokens), jnp.bfloat16),
            pltpu.VMEM((rows, dl), jnp.float32),
            pltpu.VMEM((rows, 128), jnp.float32),
            pltpu.VMEM((rows, width), jnp.bfloat16),
        ],
        compiler_params=pltpu.CompilerParams(vmem_limit_bytes=56 * 2 ** 20),
    )(previous, latent_kv, queries, w_uk, w_uv, grad_out)


def shift(array, axis, by):
    peers = lax.axis_size(axis)
    return lax.ppermute(array, axis, [(i, i + by) for i in range(peers) if 0 <= i + by < peers])


MESH = pl.DeviceIdType.MESH


def reduce_kernel(
    part_ref, final_ref, out_ref, r1, r1e, r2, r2e, s2, s2e, eout, ein,
    ss1, rs1, ss1e, rs1e, ss2, rs2, ss2e, rs2e, sse, rse, ctxs=1, heads=2,
):
    c = lax.axis_index("ctx")
    h = lax.axis_index("head")
    m0, core = h // 2, h % 2
    half = heads // 2
    blk = out_ref.shape[0]
    tokens = blk * heads
    er = W // heads
    per = blk // er
    sib = m0 * 2 + 1 - core
    away = tokens - W + h * er
    dest = away // blk
    slot = (away % blk) // er
    takes = jnp.logical_and(h * blk >= tokens - W, c < ctxs - 1)
    gives = c > 0
    giver = jnp.maximum((h * blk - (tokens - W)) // er, 0)
    below = jnp.maximum(c - 1, 0)
    above = jnp.minimum(c + 1, ctxs - 1)

    barrier = pltpu.get_barrier_semaphore()

    def greet(cc, hh):
        pl.semaphore_signal(barrier, inc=1, device_id=(cc, hh), device_id_type=MESH)

    greet(c, sib)
    for k in range(half - 1):
        greet(c, ((m0 + 1 + k) % half) * 2 + core)

    @pl.when(gives)
    def _():
        greet(below, dest)

    @pl.when(takes)
    def _():
        for i in range(per):
            greet(above, giver + i)

    pl.semaphore_wait(
        barrier, half + gives.astype(jnp.int32) + per * takes.astype(jnp.int32)
    )

    def rows_of(m, parity, size, base):
        return pl.ds(pl.multiple_of(base + (2 * m + parity) * size, 16), size)

    def remote(src, dst, send, recv, cc, hh):
        return pltpu.make_async_remote_copy(
            src_ref=src, dst_ref=dst, send_sem=send, recv_sem=recv,
            device_id=(cc, hh), device_id_type=MESH,
        )

    first = {}
    for name, size, base, land, sends, recvs in (
        ("e", er, 0, r1e, ss1e, rs1e), ("o", blk, W, r1, ss1, rs1),
    ):
        for k in range(half):
            m = (m0 + 1 + k) % half
            cp = remote(
                part_ref.at[rows_of(m, 1 - core, size, base)], land.at[k],
                sends.at[k], recvs.at[k], c, sib,
            )
            cp.start()
            first[name, k] = cp

    second = {}
    kept = {}
    for name, size, base, land, out, land2, sends, recvs in (
        ("e", er, 0, r1e, s2e, r2e, ss2e, rs2e), ("o", blk, W, r1, s2, r2, ss2, rs2),
    ):
        for k in range(half):
            m = (m0 + 1 + k) % half
            first[name, k].wait_recv()
            both = part_ref[rows_of(m, core, size, base), :].astype(jnp.float32)
            both = both + land[k].astype(jnp.float32)
            if k == half - 1:
                if name == "e":
                    eout[...] = both
                else:
                    out_ref[...] = both
            else:
                out[k] = both.astype(jnp.bfloat16)
                cp = remote(out.at[k], land2.at[k], sends.at[k], recvs.at[k], c, 2 * m + core)
                cp.start()
                second[name, k] = cp

    for k in range(half - 1):
        second["e", k].wait_recv()
    edge = eout[...]
    for k in range(half - 1):
        edge = edge + r2e[k].astype(jnp.float32)
    s2e[half - 1] = edge.astype(jnp.bfloat16)

    @pl.when(gives)
    def _():
        remote(s2e.at[half - 1], ein.at[slot], sse, rse.at[slot], below, dest).start()

    total = out_ref[...]
    for k in range(half - 1):
        second["o", k].wait_recv()
        total = total + r2[k].astype(jnp.float32)
    out_ref[...] = total

    @pl.when(takes)
    def _():
        for i in range(per):
            remote(s2e.at[half - 1], ein.at[i], sse, rse.at[i], above, h).wait_recv()
            out_ref[i * er:(i + 1) * er, :] += ein[i].astype(jnp.float32)

    final_ref[...] = out_ref[...].T

    for cp in first.values():
        cp.wait_send()
    for cp in second.values():
        cp.wait_send()

    @pl.when(gives)
    def _():
        remote(s2e.at[half - 1], ein.at[slot], sse, rse.at[slot], below, dest).wait_send()


def reduce_part(part, tokens):
    ctxs, heads = lax.axis_size("ctx"), lax.axis_size("head")
    width = part.shape[1]
    half, blk, er = heads // 2, tokens // heads, W // heads
    dma = pltpu.SemaphoreType.DMA
    vm = lambda n, rows: pltpu.VMEM((n, rows, width), jnp.bfloat16)
    return pl.pallas_call(
        functools.partial(reduce_kernel, ctxs=ctxs, heads=heads),
        out_shape=jax.ShapeDtypeStruct((width, blk), jnp.float32),
        in_specs=[pl.BlockSpec(memory_space=pltpu.VMEM)],
        out_specs=pl.BlockSpec(memory_space=pltpu.VMEM),
        scratch_shapes=[
            pltpu.VMEM((blk, width), jnp.float32),
            vm(half, blk), vm(half, er), vm(half, blk), vm(half, er),
            vm(half, blk), vm(half, er),
            pltpu.VMEM((er, width), jnp.float32),
            vm(blk // er, er),
            dma((half,)), dma((half,)), dma((half,)), dma((half,)),
            dma((half,)), dma((half,)), dma((half,)), dma((half,)),
            dma, dma((blk // er,)),
        ],
        compiler_params=pltpu.CompilerParams(
            collective_id=0, has_side_effects=True, vmem_limit_bytes=32 * 2 ** 20
        ),
    )(part)


def shards(queries, latent_kv, w_uk, w_uv, grad_out):
    tokens = queries.shape[0]
    latent_t = latent_kv.T
    previous = shift(latent_t[:, tokens - W:], "ctx", 1)
    grad_queries, part = attend(previous, latent_t, queries, w_uk, w_uv, grad_out)
    return grad_queries, reduce_part(part, tokens).T


def solution(mesh):
    in_specs = (
        P("ctx", "head"),
        P("ctx", None),
        P("head", None, None),
        P("head", None, None),
        P("ctx", "head"),
    )
    out_specs = (P("ctx", "head"), P(("ctx", "head"), None))
    return jax.shard_map(shards, mesh=mesh, in_specs=in_specs, out_specs=out_specs, check_vma=False)
```

```python
import functools
import math

import jax
import jax.numpy as jnp
from jax import lax
from jax.experimental import pallas as pl
from jax.experimental.pallas import tpu as pltpu
from jax.sharding import PartitionSpec as P

W = 512
T = 256
NEG = -1e30
NT = (((1,), (1,)), ((), ()))
NN = (((1,), (0,)), ((), ()))


def mm(a, b, dims=NN):
    return lax.dot_general(a, b, dims, preferred_element_type=jnp.float32)


def attend_kernel(*refs, behind):
    prev_ref, own_ref, q_ref, uk_ref, uv_ref, g_ref = refs[:6]
    if behind:
        later_ref = refs[6]
        refs = refs[2:]
    gq_ref, part_ref, kcat, kt, vs, pt, dst, acc, racc, lats = refs[6:]
    step = pl.program_id(0)
    tokens = q_ref.shape[0]
    tiles = tokens // T
    reach = W // T
    chunks = tiles + reach
    dl = uk_ref.shape[1]
    scale = 192 ** -0.5
    c2 = scale * math.log2(math.e)
    first_bias = jnp.where(lax.axis_index("ctx") == 0, NEG, 0.0).astype(jnp.float32)

    @pl.when(step == 0)
    def _():
        acc[...] = jnp.zeros_like(acc)
        racc[...] = jnp.zeros_like(racc)
        for j in range(chunks):
            ref, i = (prev_ref, j) if j < reach else (own_ref, j - reach)
            lats[j * T:(j + 1) * T, :] = ref[:, i * T:(i + 1) * T].T

    wk = jnp.concatenate([uk_ref[0], uk_ref[1]], axis=1)
    wv = jnp.concatenate([uv_ref[0], uv_ref[1]], axis=1)
    wall = jnp.concatenate([wk, wv], axis=1)
    zero64 = jnp.zeros((T, 64), jnp.float32)
    zero128 = jnp.zeros((T, 128), jnp.float32)

    for j in range(chunks):
        rows = slice(j * T, (j + 1) * T)
        lat = lats[rows, :]
        kr = lat[:, dl:].astype(jnp.float32)
        k2 = mm(lat[:, :dl], wk)
        v2 = mm(lat[:, :dl], wv)
        ka = jnp.concatenate([k2[:, :128], kr, zero64], axis=1).astype(jnp.bfloat16)
        kb = pltpu.roll(jnp.concatenate([k2[:, 128:], kr, zero64], axis=1), 64, 1).astype(jnp.bfloat16)
        kcat[0, rows, :] = ka
        kcat[1, rows, :] = kb
        kt[0, :, rows] = ka.T
        kt[1, :, rows] = kb.T
        vs[rows, :] = v2.astype(jnp.bfloat16)

    u = lax.broadcasted_iota(jnp.int32, (T, T), 0)
    r = lax.broadcasted_iota(jnp.int32, (T, T), 1)
    low_keep = u > r
    lane = lax.broadcasted_iota(jnp.int32, (T, 128), 1)

    def tile(t, e):
        qrows = slice(t * T, (t + 1) * T)
        q = q_ref[qrows, e * 128:e * 128 + 256]
        g = g_ref[qrows, e * 128:e * 128 + 128]
        ss = []
        for a in range(reach + 1):
            rows = slice((t + a) * T, (t + a + 1) * T)
            s = mm(kcat[e, rows, :], q, NT)
            if a == 0:
                s = jnp.where(low_keep, s, NEG)
            if a == reach:
                s = jnp.where(low_keep, NEG, s)
            if behind and t + a < reach:
                s = s + first_bias
            ss.append(s)
        peak = jnp.max(ss[0], axis=0, keepdims=True)
        for s in ss[1:]:
            peak = jnp.maximum(peak, jnp.max(s, axis=0, keepdims=True))
        es = [jnp.exp2((s - peak) * c2) for s in ss]
        total = sum(jnp.sum(x, axis=0, keepdims=True) for x in es)
        inv = 1.0 / total
        ds_list = []
        dps = []
        delta = jnp.zeros((1, T), jnp.float32)
        for a in range(reach + 1):
            rows = slice((t + a) * T, (t + a + 1) * T)
            dp = mm(vs[rows, e * 128:e * 128 + 128], g, NT)
            dps.append(dp)
            delta = delta + jnp.sum(es[a] * dp, axis=0, keepdims=True)
        delta = delta * inv
        dq = jnp.zeros((256, T), jnp.float32)
        for a in range(reach + 1):
            rows = slice((t + a) * T, (t + a + 1) * T)
            p = es[a] * inv
            pt[e, rows, qrows] = p.astype(jnp.bfloat16)
            ds = (p * (dps[a] - delta)).astype(jnp.bfloat16)
            dst[e, rows, qrows] = ds
            ds_list.append(ds)
        dq = mm(kt[e, :, t * T:(t + reach + 1) * T], jnp.concatenate(ds_list, axis=0))
        return (dq * scale).T

    def chunk(j):
        rows = slice(j * T, (j + 1) * T)
        t0, t1 = max(0, j - reach), min(tiles - 1, j)
        qrows = slice(t0 * T, (t1 + 1) * T)
        dka = mm(dst[0, rows, qrows], q_ref[qrows, 0:256]) * scale
        dkb = mm(dst[1, rows, qrows], q_ref[qrows, 128:384]) * scale
        dva = mm(pt[0, rows, qrows], g_ref[qrows, 0:128])
        dvb = mm(pt[1, rows, qrows], g_ref[qrows, 128:256])
        racc[rows, :] += jnp.where(lane < 64, dka[:, 128:], dkb[:, 128:])
        dkb = pltpu.roll(dkb, 192, 1)[:, :128]
        grads = jnp.concatenate(
            [dka[:, :128], dkb, dva, dvb], axis=1
        ).astype(jnp.bfloat16)
        acc[rows, :] += mm(grads, wall, NT)

    for t in range(tiles):
        qrows = slice(t * T, (t + 1) * T)
        a = tile(t, 0)
        b = tile(t, 1)
        gq_ref[qrows, 0:128] = a[:, :128].astype(jnp.bfloat16)
        gq_ref[qrows, 128:256] = (a[:, 128:] + b[:, :128]).astype(jnp.bfloat16)
        gq_ref[qrows, 256:384] = b[:, 128:].astype(jnp.bfloat16)
        chunk(t)
    for j in range(tiles, chunks):
        chunk(j)

    @pl.when(step == pl.num_programs(0) - 1)
    def _():
        rope = racc[:, :64] + racc[:, 64:]
        if not behind:
            part_ref[:, :dl] = acc[...].astype(part_ref.dtype)
            part_ref[:, dl:] = rope.astype(part_ref.dtype)
        else:
            part_ref[:W, :dl] = acc[:W, :].astype(part_ref.dtype)
            part_ref[:W, dl:] = rope[:W].astype(part_ref.dtype)
            later = later_ref[:W, :].astype(jnp.float32)
            part_ref[W:2 * W, :dl] = (acc[W:, :] + later[:, :dl]).astype(part_ref.dtype)
            part_ref[W:2 * W, dl:] = (rope[W:] + later[:, dl:]).astype(part_ref.dtype)
            part_ref[2 * W:, :] = later_ref[W:, :]


def attend(previous, latent_t, queries, w_uk, w_uv, grad_out, later=None, grads=None):
    behind = later is not None
    tokens = W
    place = 0 if behind else 1
    heads = w_uk.shape[0]
    dl = w_uk.shape[1]
    rows = tokens + W
    width = latent_t.shape[0]
    full = lambda s: pl.BlockSpec(s, lambda i: (0,) * len(s))
    in_specs = [
        full((width, W)),
        pl.BlockSpec((width, tokens), lambda i: (0, place)),
        pl.BlockSpec((tokens, 384), lambda i: (place, i)),
        pl.BlockSpec((2, dl, 128), lambda i: (i, 0, 0)),
        pl.BlockSpec((2, dl, 128), lambda i: (i, 0, 0)),
        pl.BlockSpec((tokens, 256), lambda i: (place, i)),
    ]
    operands = [previous, latent_t, queries, w_uk, w_uv, grad_out]
    if behind:
        in_specs += [full(later.shape), pl.BlockSpec(memory_space=pl.ANY)]
        operands += [later, grads]
    part_rows = rows + W if behind else rows
    return pl.pallas_call(
        functools.partial(attend_kernel, behind=behind),
        grid=(heads // 2,),
        in_specs=in_specs,
        out_specs=[
            pl.BlockSpec((tokens, 384), lambda i: (place, i)),
            full((part_rows, width)),
        ],
        out_shape=[
            jax.ShapeDtypeStruct(queries.shape, jnp.bfloat16),
            jax.ShapeDtypeStruct((part_rows, width), jnp.bfloat16),
        ],
        input_output_aliases={7: 0} if behind else {},
        cost_estimate=pl.CostEstimate(
            flops=heads * 2 * 10 ** 9, bytes_accessed=16 * 10 ** 6, transcendentals=0
        ),
        scratch_shapes=[
            pltpu.VMEM((2, rows, 256), jnp.bfloat16),
            pltpu.VMEM((2, 256, rows), jnp.bfloat16),
            pltpu.VMEM((rows, 256), jnp.bfloat16),
            pltpu.VMEM((2, rows, tokens), jnp.bfloat16),
            pltpu.VMEM((2, rows, tokens), jnp.bfloat16),
            pltpu.VMEM((rows, dl), jnp.float32),
            pltpu.VMEM((rows, 128), jnp.float32),
            pltpu.VMEM((rows, width), jnp.bfloat16),
        ],
        compiler_params=pltpu.CompilerParams(vmem_limit_bytes=56 * 2 ** 20),
    )(*operands)


def shift(array, axis, by):
    peers = lax.axis_size(axis)
    return lax.ppermute(array, axis, [(i, i + by) for i in range(peers) if 0 <= i + by < peers])


MESH = pl.DeviceIdType.MESH


def reduce_kernel(
    part_ref, final_ref, out_ref, r1, r1e, r2, r2e, s2, s2e, eout, ein,
    ss1, rs1, ss1e, rs1e, ss2, rs2, ss2e, rs2e, sse, rse, ctxs=1, heads=2,
):
    c = lax.axis_index("ctx")
    h = lax.axis_index("head")
    m0, core = h // 2, h % 2
    half = heads // 2
    blk = out_ref.shape[0]
    tokens = blk * heads
    er = W // heads
    per = blk // er
    sib = m0 * 2 + 1 - core
    away = tokens - W + h * er
    dest = away // blk
    slot = (away % blk) // er
    takes = jnp.logical_and(h * blk >= tokens - W, c < ctxs - 1)
    gives = c > 0
    giver = jnp.maximum((h * blk - (tokens - W)) // er, 0)
    below = jnp.maximum(c - 1, 0)
    above = jnp.minimum(c + 1, ctxs - 1)

    barrier = pltpu.get_barrier_semaphore()

    def greet(cc, hh):
        pl.semaphore_signal(barrier, inc=1, device_id=(cc, hh), device_id_type=MESH)

    greet(c, sib)
    for k in range(half - 1):
        greet(c, ((m0 + 1 + k) % half) * 2 + core)

    @pl.when(gives)
    def _():
        greet(below, dest)

    @pl.when(takes)
    def _():
        for i in range(per):
            greet(above, giver + i)

    pl.semaphore_wait(
        barrier, half + gives.astype(jnp.int32) + per * takes.astype(jnp.int32)
    )

    def rows_of(m, parity, size, base):
        return pl.ds(pl.multiple_of(base + (2 * m + parity) * size, 16), size)

    def remote(src, dst, send, recv, cc, hh):
        return pltpu.make_async_remote_copy(
            src_ref=src, dst_ref=dst, send_sem=send, recv_sem=recv,
            device_id=(cc, hh), device_id_type=MESH,
        )

    first = {}
    for name, size, base, land, sends, recvs in (
        ("e", er, 0, r1e, ss1e, rs1e), ("o", blk, W, r1, ss1, rs1),
    ):
        for k in range(half):
            m = (m0 + 1 + k) % half
            cp = remote(
                part_ref.at[rows_of(m, 1 - core, size, base)], land.at[k],
                sends.at[k], recvs.at[k], c, sib,
            )
            cp.start()
            first[name, k] = cp

    second = {}
    kept = {}
    for name, size, base, land, out, land2, sends, recvs in (
        ("e", er, 0, r1e, s2e, r2e, ss2e, rs2e), ("o", blk, W, r1, s2, r2, ss2, rs2),
    ):
        for k in range(half):
            m = (m0 + 1 + k) % half
            first[name, k].wait_recv()
            both = part_ref[rows_of(m, core, size, base), :].astype(jnp.float32)
            both = both + land[k].astype(jnp.float32)
            if k == half - 1:
                if name == "e":
                    eout[...] = both
                else:
                    out_ref[...] = both
            else:
                out[k] = both.astype(jnp.bfloat16)
                cp = remote(out.at[k], land2.at[k], sends.at[k], recvs.at[k], c, 2 * m + core)
                cp.start()
                second[name, k] = cp

    for k in range(half - 1):
        second["e", k].wait_recv()
    edge = eout[...]
    for k in range(half - 1):
        edge = edge + r2e[k].astype(jnp.float32)
    s2e[half - 1] = edge.astype(jnp.bfloat16)

    @pl.when(gives)
    def _():
        remote(s2e.at[half - 1], ein.at[slot], sse, rse.at[slot], below, dest).start()

    total = out_ref[...]
    for k in range(half - 1):
        second["o", k].wait_recv()
        total = total + r2[k].astype(jnp.float32)
    out_ref[...] = total

    @pl.when(takes)
    def _():
        for i in range(per):
            remote(s2e.at[half - 1], ein.at[i], sse, rse.at[i], above, h).wait_recv()
            out_ref[i * er:(i + 1) * er, :] += ein[i].astype(jnp.float32)

    final_ref[...] = out_ref[...].T

    for cp in first.values():
        cp.wait_send()
    for cp in second.values():
        cp.wait_send()

    @pl.when(gives)
    def _():
        remote(s2e.at[half - 1], ein.at[slot], sse, rse.at[slot], below, dest).wait_send()


def reduce_part(part, tokens):
    ctxs, heads = lax.axis_size("ctx"), lax.axis_size("head")
    width = part.shape[1]
    half, blk, er = heads // 2, tokens // heads, W // heads
    dma = pltpu.SemaphoreType.DMA
    vm = lambda n, rows: pltpu.VMEM((n, rows, width), jnp.bfloat16)
    return pl.pallas_call(
        functools.partial(reduce_kernel, ctxs=ctxs, heads=heads),
        out_shape=jax.ShapeDtypeStruct((width, blk), jnp.float32),
        in_specs=[pl.BlockSpec(memory_space=pltpu.VMEM)],
        out_specs=pl.BlockSpec(memory_space=pltpu.VMEM),
        scratch_shapes=[
            pltpu.VMEM((blk, width), jnp.float32),
            vm(half, blk), vm(half, er), vm(half, blk), vm(half, er),
            vm(half, blk), vm(half, er),
            pltpu.VMEM((er, width), jnp.float32),
            vm(blk // er, er),
            dma((half,)), dma((half,)), dma((half,)), dma((half,)),
            dma((half,)), dma((half,)), dma((half,)), dma((half,)),
            dma, dma((blk // er,)),
        ],
        compiler_params=pltpu.CompilerParams(
            collective_id=0, has_side_effects=True, vmem_limit_bytes=32 * 2 ** 20
        ),
    )(part)


def shards(queries, latent_kv, w_uk, w_uv, grad_out):
    tokens = queries.shape[0]
    latent_t = latent_kv.T
    previous = shift(latent_t[:, tokens - W:], "ctx", 1)
    grads, later = attend(latent_t, latent_t, queries, w_uk, w_uv, grad_out)
    grad_queries, part = attend(
        previous, latent_t, queries, w_uk, w_uv, grad_out, later, grads
    )
    return grad_queries, reduce_part(part, tokens).T


def solution(mesh):
    in_specs = (
        P("ctx", "head"),
        P("ctx", None),
        P("head", None, None),
        P("head", None, None),
        P("ctx", "head"),
    )
    out_specs = (P("ctx", "head"), P(("ctx", "head"), None))
    return jax.shard_map(shards, mesh=mesh, in_specs=in_specs, out_specs=out_specs, check_vma=False)
```
